256 devices in a mesh: sec: 4 (over y_lo, core), tile: 64 (over x, z, y_hi).
Axes of the slice: x: 4, y: 4 (y_hi: 2, y_lo: 2; y = y_hi * 2 + y_lo), z: 8, core: 2. Of those that a mesh axis runs over, the one named last changes fastest.
Arguments:
- increments: float32 [8, 512, 96, 512], P('sec', 'tile'), may hold values from -6 to 6
- adjoint_forcing: float32 [8, 512, 96, 512], P('sec', 'tile'), may hold values from -6 to 6
- wind: float32 [8, 512, 96], P('sec', 'tile'), may hold values from -0.4 to 0.4
- coupling: float32 [512, 512], replicated, may hold values from -0.125 to 0.125
Outputs:
- model_misfit: float32 [8, 512, 96, 512], P('sec', 'tile')
- adjoint_misfit: float32 [8, 512, 96, 512], P('sec', 'tile')
The draws below stay inside these ranges and needn't reach their ends.
All inputs are finite; a program needn't handle non-finite values.
Results may differ from the reference program's by a relative error of at most 0.0001.
Values sent between devices are 32-bit elements; how exact they have to be, the bound alone decides.
A program may use at most 128 MiB of HBM per device.

```python
import jax
import jax.numpy as jnp
from jax import lax

K = 512
LAT = 96
NLON = 512
WIN = 8
STEPS = 4


def draw_wind(key, part):
    key = jax.random.fold_in(key, 7)
    sign_key, size_key = jax.random.split(key)
    shape = (WIN, NLON, LAT)
    signs = (2 * jax.random.randint(sign_key, shape, 0, 2) - 1).astype(jnp.float32)
    unit = jax.random.uniform(size_key, shape, jnp.float32)
    magnitude = 0.3 + 0.1 * unit
    return jnp.clip(signs * magnitude, -0.4, 0.4)


def block_scale(rng, shape, pieces, low, high):
    factor_of = 1.0
    for axis_at, blocks in pieces:
        draws = jax.random.uniform(jax.random.fold_in(jax.random.fold_in(rng, 6), axis_at), (blocks,), jnp.float32, low / len(pieces), high / len(pieces))
        factor_of = factor_of * jnp.repeat(jnp.exp(draws), shape[axis_at] // blocks).reshape((-1,) + (1,) * (len(shape) - 1 - axis_at))
    return factor_of


def centred(rng, shape, scale, bound, shards=(), dtype=jnp.bfloat16):
    values = jax.random.normal(rng, shape, jnp.float32) * scale
    if len(shards) > 0:
        values = block_scale(rng, shape, shards, -0.22, 0.18) * values
    return jnp.clip(values, min=-bound, max=bound).astype(dtype)


def setup_inputs(seed: int = 0) -> dict:
    key_of = jax.random.split(jax.random.key(seed), 5)
    return {
        "increments": centred(key_of[0], (WIN, NLON, LAT, K), 1.0, 6.0, ((0, 4), (1, 64)), jnp.float32),
        "adjoint_forcing": centred(key_of[1], (WIN, NLON, LAT, K), 1.0, 6.0, ((0, 4), (1, 64)), jnp.float32),
        "wind": draw_wind(jax.random.fold_in(key_of[4], 71), 0),
        "coupling": centred(key_of[3], (K, K), (4 * K) ** -0.5, 0.125, (), jnp.float32),
    }


diffusion_rate = 0.15


def lat_laplace(field):
    padded = jnp.pad(field, [(0, 0)] * (field.ndim - 2) + [(1, 1), (0, 0)])
    return padded[..., 2:, :] + padded[..., :-2, :] - 2.0 * field


def tangent_model(state, speed, coupling):
    for segment in range(STEPS):
        east_side = jnp.roll(state, -1, axis=0)
        west_side = jnp.roll(state, 1, axis=0)
        mixed = jnp.einsum("kj,xyj->xyk", coupling, state, precision=lax.Precision.HIGHEST)
        state = state + mixed - speed[:, :, None] * (east_side - west_side) + diffusion_rate * lat_laplace(state)
    return state


def adjoint_model(costate, speed, coupling):
    for segment in range(STEPS):
        pushed = speed[:, :, None] * costate
        mixed = jnp.einsum("jk,xyj->xyk", coupling, costate, precision=lax.Precision.HIGHEST)
        costate = costate + mixed + (jnp.roll(pushed, -1, axis=0) - jnp.roll(pushed, 1, axis=0)) + diffusion_rate * lat_laplace(costate)
    return costate


def reference(increments, adjoint_forcing, wind, coupling):
    forward_end = lax.map(lambda pair: tangent_model(pair[0], pair[1], coupling), (increments, wind))
    backward_end = lax.map(lambda pair: adjoint_model(pair[0], pair[1], coupling), (adjoint_forcing, wind))
    zeros_one = jnp.zeros_like(increments[:1])
    model_misfit = increments - jnp.concatenate([zeros_one, forward_end[:-1]], 0)
    adjoint_misfit = adjoint_forcing - jnp.concatenate([backward_end[1:], zeros_one], 0)
    return model_misfit, adjoint_misfit
```

```python
import functools

import jax
import jax.numpy as jnp
from jax import lax
from jax.experimental import pallas as pl
from jax.experimental.pallas import tpu as pltpu
from jax.sharding import PartitionSpec as P

MESH = pl.DeviceIdType.MESH
STEPS = 4
DIFFUSION = 0.15


def halves(x):
    high = x.astype(jnp.bfloat16)
    return high, (x - high.astype(jnp.float32)).astype(jnp.bfloat16)


def dot(a, b):
    return jnp.dot(a, b, preferred_element_type=jnp.float32)


def when(condition):
    return (lambda f: f()) if condition is None else pl.when(condition)


def kernel(
    inc, forc, wind, coupling, model, adjoint,
    state, result, last, winds, speed, matrices, send, recv, wsend, wrecv, base_sem, out_sem, last_sem,
):
    sections, tiles = lax.axis_size("sec"), lax.axis_size("tile")
    sec, tile = lax.axis_index("sec"), lax.axis_index("tile")
    east, west = lax.rem(tile + 1, tiles), lax.rem(tile + tiles - 1, tiles)
    width, lats, size = inc.shape[1:]
    wide = width + 2 * STEPS
    has_next, has_previous = sec < sections - 1, sec > 0

    local = [
        pltpu.make_async_copy(inc.at[0], state.at[2, pl.ds(STEPS, width)], recv.at[2, STEPS]),
        pltpu.make_async_copy(forc.at[1], state.at[3, pl.ds(STEPS, width)], recv.at[3, STEPS]),
    ]
    bases = [
        pltpu.make_async_copy(source, result.at[unit], base_sem.at[unit])
        for unit, source in enumerate((inc.at[0], forc.at[1], inc.at[1], forc.at[0]))
    ]

    barrier = pltpu.get_barrier_semaphore()
    for to, condition in ((sec, None), (sec + 1, has_next), (sec - 1, has_previous)):
        for t in (east, west) if condition is None else (east, west, tile):
            @when(condition)
            def _():
                pl.semaphore_signal(barrier, inc=1, device_id=(to, t), device_id_type=MESH)

    def remote(source, target, sems, at, device):
        return pltpu.make_async_remote_copy(
            src_ref=source, dst_ref=target, send_sem=sems[0].at[at], recv_sem=sems[1].at[at],
            device_id=device, device_id_type=MESH,
        )

    def wind_copies(unit, window, section, parts):
        to = {0: east, 1: tile, 2: west}
        return [
            remote(wind.at[window], winds.at[unit, pl.ds(8 * part, 8)], (wsend, wrecv), (unit, part), (section, to[part]))
            for part in parts
        ]

    def halo(unit, source, section, part, first, count):
        if part == 0:
            at, column, to = STEPS - first - count, width - first - count, east
        else:
            at, column, to = STEPS + width + first, first, west
        return remote(
            source.at[pl.ds(column, count)], state.at[unit, pl.ds(at, count)], (send, recv), (unit, at), (section, to)
        )

    def start_of(unit, source, section):
        return remote(
            source, state.at[unit, pl.ds(STEPS, width)], (send, recv), (unit, STEPS), (section, tile)
        )

    ahead = (has_next, has_previous)
    behind = (has_previous, has_next)
    copies = []
    copies += [(c, *ahead) for c in wind_copies(0, 1, sec + 1, (1, 0, 2))]
    copies += [(c, *behind) for c in wind_copies(1, 0, sec - 1, (1, 0, 2))]
    copies += [(c, None, None) for c in wind_copies(2, 0, sec, (0, 2)) + wind_copies(3, 1, sec, (0, 2))]
    copies += [(start_of(0, inc.at[1], sec + 1), *ahead)]
    copies += [(start_of(1, forc.at[0], sec - 1), *behind)]
    copies += [(halo(0, inc.at[1], sec + 1, part, 0, STEPS), *ahead) for part in (0, 1)]
    copies += [(halo(1, forc.at[0], sec - 1, part, 0, STEPS), *behind) for part in (0, 1)]
    copies += [(halo(2, inc.at[0], sec, part, 0, STEPS), None, None) for part in (0, 1)]
    near = [[halo(3, forc.at[1], sec, part, j, 1) for part in (0, 1)] for j in range(STEPS - 1)]
    copies += [(c, None, None) for pair in near for c in pair]
    far = [
        remote(forc.at[1, column], last.at[part], (last_sem.at[0], last_sem.at[1]), part, (sec, to))
        for part, column, to in ((0, width - STEPS, east), (1, STEPS - 1, west))
    ]
    copies += [(c, None, None) for c in far]

    for c in local + bases:
        c.start()
    pl.semaphore_wait(barrier, 8 - 3 * ((sec + 1) // sections) - 3 * ((sections - sec) // sections))
    for c, sends, _ in copies:
        @when(sends)
        def _():
            c.start()

    for at, matrix in enumerate((coupling[...].T, coupling[...])):
        high, low = halves(matrix)
        matrices[2 * at] = high
        matrices[2 * at + 1] = low
    zero = jnp.zeros((lats, size), jnp.float32)
    state[3, 0] = zero
    state[3, wide - 1] = zero
    winds[2, pl.ds(8, 8)] = wind[0]
    winds[3, pl.ds(8, 8)] = wind[1]

    def active(unit):
        return jnp.logical_not(((unit == 0) & (sec == 0)) | ((unit == 1) & (sec == sections - 1)))

    def wait_wind(unit, part):
        remote(wind.at[0], winds.at[unit, pl.ds(8 * part, 8)], (wsend, wrecv), (unit, part), (sec, east)).wait_recv()

    def spread(unit, _):
        @pl.when(active(unit))
        def _():
            wait_wind(unit, 0)
            wait_wind(unit, 2)

            @pl.when(unit < 2)
            def _():
                wait_wind(unit, 1)

            turned = winds[unit].T * jnp.where(unit % 2 == 0, 1.0, -1.0)
            for column in range(wide):
                speed[unit, column] = jnp.broadcast_to(turned[:, column + 4 : column + 5], (lats, 128))
        return 0

    lax.fori_loop(0, 4, spread, 0)

    lat = lax.broadcasted_iota(jnp.int32, (lats, size), 0)

    def flow(unit, column):
        return jnp.concatenate([speed[unit, column]] * (size // 128), 1)

    def update(unit, step, column):
        base = jnp.where(unit == 3, 4 + STEPS - 1, 4)
        source = jnp.where(step == 1, unit, base + step - 2)
        shift = unit % 2
        columns = (column, wide - 1 - column)
        centre = [state[source, at] for at in columns]
        high, low = halves(jnp.concatenate(centre, 0))
        coarse, fine = matrices[2 * shift], matrices[2 * shift + 1]
        mixed = dot(high, coarse) + dot(low, coarse) + dot(high, fine)
        for i, at in enumerate(columns):
            x = centre[i]
            north = jnp.where(lat == lats - 1, 0.0, pltpu.roll(x, lats - 1, 0))
            south = jnp.where(lat == 0, 0.0, pltpu.roll(x, 1, 0))
            value = (
                (1 - 2 * DIFFUSION) * x
                + mixed[i * lats : (i + 1) * lats]
                + flow(unit, at - shift) * state[source, at - 1]
                - flow(unit, at + shift) * state[source, at + 1]
                + DIFFUSION * (north + south)
            )

            @pl.when(step < STEPS)
            def _():
                state[base + step - 1, at] = value

            @pl.when(step == STEPS)
            def _():
                result[unit, at - STEPS] -= value

    def outgoing(unit):
        target = (model.at[0], adjoint.at[1], model.at[1], adjoint.at[0])[unit]
        return pltpu.make_async_copy(result.at[unit], target, out_sem.at[unit])

    local[1].wait()
    half = wide // 2

    def inner(step, _):
        def columns(column, _):
            update(3, step, column)
            return 0

        return lax.fori_loop(STEPS + step, half, columns, 0)

    lax.fori_loop(1, STEPS, inner, 0)
    for c in bases:
        c.wait()

    def whole(unit, _):
        @pl.when(active(unit))
        def _():
            for at, count in ((STEPS, width), (0, STEPS), (STEPS + width, STEPS)):
                remote(
                    inc.at[0, pl.ds(0, count)], state.at[unit, pl.ds(at, count)], (send, recv), (unit, at), (sec, east)
                ).wait_recv()

            def steps(step, _):
                def columns(column, _):
                    update(unit, step, column)
                    return 0

                return lax.fori_loop(step, half, columns, 0)

            lax.fori_loop(1, STEPS + 1, steps, 0)

        return 0

    lax.fori_loop(0, 3, whole, 0)
    for unit in range(3):
        outgoing(unit).start()

    def waves(j, _):
        @pl.when(j < STEPS)
        def _():
            for at in (STEPS - j, STEPS + width - 1 + j):
                remote(
                    forc.at[1, pl.ds(0, 1)], state.at[3, pl.ds(at, 1)], (send, recv), (3, at), (sec, east)
                ).wait_recv()

        def steps(step, _):
            update(3, step, STEPS - j + step)
            return 0

        return lax.fori_loop(1, STEPS + 1, steps, 0)

    lax.fori_loop(1, STEPS + 1, waves, 0)

    for part in (0, 1):
        reach = functools.reduce(
            jnp.multiply, [flow(3, step - 1 if part == 0 else wide - step) for step in range(1, STEPS + 1)]
        )
        far[part].wait_recv()
        result[3, 0 if part == 0 else width - 1] -= reach * last[part]
    outgoing(3).start()

    for c, sends, _ in copies:
        @when(sends)
        def _():
            c.wait_send()
    for unit in range(4):
        outgoing(unit).wait()


def solution(mesh):
    def body(increments, adjoint_forcing, wind, coupling):
        _, width, lats, size = increments.shape
        wide = width + 2 * STEPS
        any_space = pl.BlockSpec(memory_space=pl.ANY)
        vmem = pl.BlockSpec(memory_space=pltpu.VMEM)
        shape = jax.ShapeDtypeStruct(increments.shape, jnp.float32)
        return pl.pallas_call(
            kernel,
            out_shape=(shape, shape),
            in_specs=[any_space, any_space, vmem, vmem],
            out_specs=(any_space, any_space),
            scratch_shapes=[
                pltpu.VMEM((4 + 2 * (STEPS - 1), wide, lats, size), jnp.float32),
                pltpu.VMEM((4, width, lats, size), jnp.float32),
                pltpu.VMEM((2, lats, size), jnp.float32),
                pltpu.VMEM((4, 3 * width, lats), jnp.float32),
                pltpu.VMEM((4, wide, lats, 128), jnp.float32),
                pltpu.VMEM((4, size, size), jnp.bfloat16),
                pltpu.SemaphoreType.DMA((4, wide)),
                pltpu.SemaphoreType.DMA((4, wide)),
                pltpu.SemaphoreType.DMA((4, 3)),
                pltpu.SemaphoreType.DMA((4, 3)),
                pltpu.SemaphoreType.DMA((4,)),
                pltpu.SemaphoreType.DMA((4,)),
                pltpu.SemaphoreType.DMA((2, 2)),
            ],
            compiler_params=pltpu.CompilerParams(
                collective_id=0, has_side_effects=True, vmem_limit_bytes=56 * 2**20
            ),
        )(increments, adjoint_forcing, wind, coupling)

    in_specs = (
        P("sec", "tile", None, None),
        P("sec", "tile", None, None),
        P("sec", "tile", None),
        P(),
    )
    out_specs = (P("sec", "tile", None, None), P("sec", "tile", None, None))
    return jax.shard_map(body, mesh=mesh, in_specs=in_specs, out_specs=out_specs, check_vma=False)
```

```python
import functools

import jax
import jax.numpy as jnp
from jax import lax
from jax.experimental import pallas as pl
from jax.experimental.pallas import tpu as pltpu
from jax.sharding import PartitionSpec as P

MESH = pl.DeviceIdType.MESH
STEPS = 4
DIFFUSION = 0.15
FIRST = 12
LATER = ((0, (12, 13)), (1, (14, 15)))


def level(step):
    return 15 * step - step * (step - 1)


def halves(x):
    high = x.astype(jnp.bfloat16)
    return high, (x - high.astype(jnp.float32)).astype(jnp.bfloat16)


def dot(a, b):
    return jnp.dot(a, b, preferred_element_type=jnp.float32)


def when(condition):
    return (lambda f: f()) if condition is None else pl.when(condition)


def kernel(
    inc, forc, wind, coupling, model, adjoint,
    state, result, last, winds, speed, matrices, send, recv, wsend, wrecv, base_sem, out_sem, last_sem,
):
    sections, tiles = lax.axis_size("sec"), lax.axis_size("tile")
    sec, tile = lax.axis_index("sec"), lax.axis_index("tile")
    east, west = lax.rem(tile + 1, tiles), lax.rem(tile + tiles - 1, tiles)
    width, lats, size = inc.shape[1:]
    wide = width + 2 * STEPS
    has_next, has_previous = sec < sections - 1, sec > 0

    local = [
        pltpu.make_async_copy(source.at[pl.ds(at, 2)], state.at[unit, pl.ds(STEPS + at, 2)], recv.at[unit, STEPS + at])
        for unit, source in ((0, inc.at[0]), (3, forc.at[1]))
        for at in range(0, width, 2)
    ]
    bases = [
        pltpu.make_async_copy(source, result.at[unit], base_sem.at[unit])
        for unit, source in enumerate((inc.at[1], forc.at[1], inc.at[0], forc.at[0]))
    ]

    barrier = pltpu.get_barrier_semaphore()
    for to, condition in ((sec, None), (sec + 1, has_next), (sec - 1, has_previous)):
        for t in (east, west) if condition is None else (east, west, tile):
            @when(condition)
            def _():
                pl.semaphore_signal(barrier, inc=1, device_id=(to, t), device_id_type=MESH)

    def remote(source, target, sems, at, device):
        return pltpu.make_async_remote_copy(
            src_ref=source, dst_ref=target, send_sem=sems[0].at[at], recv_sem=sems[1].at[at],
            device_id=device, device_id_type=MESH,
        )

    def wind_copies(unit, window, section, parts):
        to = {0: east, 1: tile, 2: west}
        return [
            remote(wind.at[window], winds.at[unit, pl.ds(8 * part, 8)], (wsend, wrecv), (unit, part), (section, to[part]))
            for part in parts
        ]

    def halo(unit, source, section, part, first, count):
        if part == 0:
            at, column, to = STEPS - first - count, width - first - count, east
        else:
            at, column, to = STEPS + width + first, first, west
        return remote(
            source.at[pl.ds(column, count)], state.at[unit, pl.ds(at, count)], (send, recv), (unit, at), (section, to)
        )

    def start_of(unit, source, section, at):
        return remote(
            source.at[pl.ds(at, 2)], state.at[unit, pl.ds(STEPS + at, 2)], (send, recv), (unit, STEPS + at), (section, tile)
        )

    def pair(unit, j):
        source, to, sends = (
            (inc.at[0], sec, None), (forc.at[0], sec - 1, has_previous), (inc.at[1], sec + 1, has_next), (forc.at[1], sec, None)
        )[unit]
        return [(halo(unit, source, to, part, j - 1, 1), sends) for part in (0, 1)]

    def far(at):
        source = (inc.at[0], forc.at[1])[at]
        return [
            (remote(source.at[column], last.at[at, part], (last_sem.at[0], last_sem.at[1]), (at, part), (sec, to)), None)
            for part, column, to in ((0, width - STEPS, east), (1, STEPS - 1, west))
        ]

    small = [(c, None) for c in wind_copies(0, 0, sec, (0, 2)) + wind_copies(3, 1, sec, (0, 2))]
    small += [(c, has_previous) for c in wind_copies(1, 0, sec - 1, (1, 0, 2))]
    small += [(c, has_next) for c in wind_copies(2, 1, sec + 1, (1, 0, 2))]
    starts = [
        [(start_of(1, forc.at[0], sec - 1, at), has_previous), (start_of(2, inc.at[1], sec + 1, at), has_next)]
        for at in range(0, width, 2)
    ]
    order = [(unit, j) for j in range(1, STEPS + 1) for unit in (1, 2)]
    order += [(unit, j) for j in range(1, STEPS) for unit in (0, 3)]
    farthest = [far(0), far(1)]
    pairs = [pair(unit, j) for unit, j in order] + farthest

    def launch(group):
        for c, sends in group:
            @when(sends)
            def _():
                c.start()

    def leave(group):
        for c, sends in group:
            @when(sends)
            def _():
                c.wait_send()

    for c in local + bases:
        c.start()
    pl.semaphore_wait(barrier, 8 - 3 * ((sec + 1) // sections) - 3 * ((sections - sec) // sections))
    launch(small)
    for at, group in enumerate(pairs[:FIRST]):
        if at % 2 == 0 and at // 2 < len(starts):
            launch(starts[at // 2])
        launch(group)

    for at, matrix in enumerate((coupling[...].T, coupling[...])):
        high, low = halves(matrix)
        matrices[2 * at] = high
        matrices[2 * at + 1] = low
    zero = jnp.zeros((lats, size), jnp.float32)
    for unit in (0, 3):
        state[unit, 0] = zero
        state[unit, wide - 1] = zero
    winds[0, pl.ds(8, 8)] = wind[0]
    winds[3, pl.ds(8, 8)] = wind[1]

    def active(unit):
        return jnp.logical_not(((unit == 1) & (sec == sections - 1)) | ((unit == 2) & (sec == 0)))

    def wait_wind(unit, part):
        remote(wind.at[0], winds.at[unit, pl.ds(8 * part, 8)], (wsend, wrecv), (unit, part), (sec, east)).wait_recv()

    def spread(unit, _):
        @pl.when(active(unit))
        def _():
            wait_wind(unit, 0)
            wait_wind(unit, 2)

            @pl.when((unit == 1) | (unit == 2))
            def _():
                wait_wind(unit, 1)

            turned = winds[unit].T * jnp.where(unit % 2 == 0, 1.0, -1.0)
            for column in range(wide):
                speed[unit, column] = jnp.broadcast_to(turned[:, column + 4 : column + 5], (lats, 128))
        return 0

    lax.fori_loop(0, 4, spread, 0)

    lat = lax.broadcasted_iota(jnp.int32, (lats, size), 0)

    def flow(unit, column):
        return jnp.concatenate([speed[unit, column]] * (size // 128), 1)

    def update(units, step, column):
        before, after = level(step - 1), level(step)
        columns = (column, wide - 1 - column)
        centres = [[state[unit, before + at] for at in columns] for unit in units]
        mixed = []
        for way, centre in enumerate(centres):
            high, low = halves(jnp.concatenate(centre, 0))
            coarse, fine = matrices[2 * way], matrices[2 * way + 1]
            mixed.append(dot(high, coarse) + dot(low, coarse) + dot(high, fine))
        values = []
        for way, unit in enumerate(units):
            for i, at in enumerate(columns):
                x = centres[way][i]
                north = jnp.where(lat == lats - 1, 0.0, pltpu.roll(x, lats - 1, 0))
                south = jnp.where(lat == 0, 0.0, pltpu.roll(x, 1, 0))
                value = (
                    (1 - 2 * DIFFUSION) * x
                    + mixed[way][i * lats : (i + 1) * lats]
                    + flow(unit, at - way) * state[unit, before + at - 1]
                    - flow(unit, at + way) * state[unit, before + at + 1]
                    + DIFFUSION * (north + south)
                )
                values.append((unit, at, value))

        @pl.when(step < STEPS)
        def _():
            for unit, at, value in values:
                state[unit, after + at] = value

        @pl.when(step == STEPS)
        def _():
            for unit, at, value in values:
                result[unit, at - STEPS] -= jnp.where(active(unit), value, 0.0)

    def outgoing(unit):
        target = (model.at[1], adjoint.at[1], model.at[0], adjoint.at[0])[unit]
        return pltpu.make_async_copy(result.at[unit], target, out_sem.at[unit])

    for c in bases:
        c.wait()
    half = wide // 2

    def arrive(unit, at, count):
        remote(
            inc.at[0, pl.ds(0, count)], state.at[unit, pl.ds(at, count)], (send, recv), (unit, at), (sec, east)
        ).wait_recv()

    def event(number, _):
        moved = (number >= 1) & (number <= STEPS)
        units = (jnp.where(moved, 2, 0), jnp.where(moved, 1, 3))
        j = jnp.where(number > STEPS, number - STEPS, number)
        opens = number <= 1
        for unit in units:
            @pl.when(active(unit))
            def _():
                @pl.when(opens)
                def _():
                    for at in range(STEPS, STEPS + width, 2):
                        arrive(unit, at, 2)

                @pl.when((j > 0) & (number < 2 * STEPS))
                def _():
                    arrive(unit, STEPS - j, 1)
                    arrive(unit, STEPS + width - 1 + j, 1)

        for at, numbers in LATER:
            @pl.when(number == at + 1)
            def _():
                for follower in numbers:
                    launch(pairs[follower])

        def wave(q, _):
            def steps(step, _):
                def columns(column, _):
                    update(units, step, column)
                    return 0

                first = STEPS - q + step
                return lax.fori_loop(first, jnp.where(q == 0, half, first + 1), columns, 0)

            return lax.fori_loop(1, STEPS + 1, steps, 0)

        lax.fori_loop(jnp.where(opens, 0, j), j + 1, wave, 0)

        @pl.when(number == STEPS)
        def _():
            outgoing(1).start()
            outgoing(2).start()

        return 0

    lax.fori_loop(0, 2 * STEPS + 1, event, 0)

    for at, unit in enumerate((0, 3)):
        for part in (0, 1):
            first = -at if part == 0 else at
            reach = functools.reduce(
                jnp.multiply, [flow(unit, (step if part == 0 else wide - 1 - step) + first) for step in range(1, STEPS + 1)]
            )
            farthest[at][part][0].wait_recv()
            result[unit, 0 if part == 0 else width - 1] -= reach * last[at, part]
        outgoing(unit).start()

    for group in [small, *starts, *pairs]:
        leave(group)
    for unit in range(4):
        outgoing(unit).wait()


def solution(mesh):
    def body(increments, adjoint_forcing, wind, coupling):
        _, width, lats, size = increments.shape
        wide = width + 2 * STEPS
        any_space = pl.BlockSpec(memory_space=pl.ANY)
        vmem = pl.BlockSpec(memory_space=pltpu.VMEM)
        shape = jax.ShapeDtypeStruct(increments.shape, jnp.float32)
        return pl.pallas_call(
            kernel,
            out_shape=(shape, shape),
            in_specs=[any_space, any_space, vmem, vmem],
            out_specs=(any_space, any_space),
            scratch_shapes=[
                pltpu.VMEM((4, level(STEPS - 1) + wide - STEPS + 1, lats, size), jnp.float32),
                pltpu.VMEM((4, width, lats, size), jnp.float32),
                pltpu.VMEM((2, 2, lats, size), jnp.float32),
                pltpu.VMEM((4, 3 * width, lats), jnp.float32),
                pltpu.VMEM((4, wide, lats, 128), jnp.float32),
                pltpu.VMEM((4, size, size), jnp.bfloat16),
                pltpu.SemaphoreType.DMA((4, wide)),
                pltpu.SemaphoreType.DMA((4, wide)),
                pltpu.SemaphoreType.DMA((4, 3)),
                pltpu.SemaphoreType.DMA((4, 3)),
                pltpu.SemaphoreType.DMA((4,)),
                pltpu.SemaphoreType.DMA((4,)),
                pltpu.SemaphoreType.DMA((2, 2, 2)),
            ],
            compiler_params=pltpu.CompilerParams(
                collective_id=0, has_side_effects=True, vmem_limit_bytes=58 * 2**20
            ),
        )(increments, adjoint_forcing, wind, coupling)

    in_specs = (
        P("sec", "tile", None, None),
        P("sec", "tile", None, None),
        P("sec", "tile", None),
        P(),
    )
    out_specs = (P("sec", "tile", None, None), P("sec", "tile", None, None))
    return jax.shard_map(body, mesh=mesh, in_specs=in_specs, out_specs=out_specs, check_vma=False)
```

```python
import functools

import jax
import jax.numpy as jnp
from jax import lax
from jax.experimental import pallas as pl
from jax.experimental.pallas import tpu as pltpu
from jax.sharding import PartitionSpec as P

MESH = pl.DeviceIdType.MESH
STEPS = 4
DIFFUSION = 0.15
FIRST = 10
LATER = ((0, (10, 11, 12, 13)), (1, (14, 15)))


def level(step):
    return 15 * step - step * (step - 1)


def halves(x):
    high = x.astype(jnp.bfloat16)
    return high, (x - high.astype(jnp.float32)).astype(jnp.bfloat16)


def dot(a, b):
    return jnp.dot(a, b, preferred_element_type=jnp.float32)


def when(condition):
    return (lambda f: f()) if condition is None else pl.when(condition)


def kernel(
    inc, forc, wind, coupling, model, adjoint,
    state, result, last, winds, speed, matrices, send, recv, wsend, wrecv, base_sem, out_sem, last_sem,
):
    sections, tiles = lax.axis_size("sec"), lax.axis_size("tile")
    sec, tile = lax.axis_index("sec"), lax.axis_index("tile")
    east, west = lax.rem(tile + 1, tiles), lax.rem(tile + tiles - 1, tiles)
    width, lats, size = inc.shape[1:]
    wide = width + 2 * STEPS
    has_next, has_previous = sec < sections - 1, sec > 0

    local = [
        pltpu.make_async_copy(source.at[pl.ds(at, 2)], state.at[unit, pl.ds(STEPS + at, 2)], recv.at[unit, STEPS + at])
        for unit, source in ((0, inc.at[0]), (3, forc.at[1]))
        for at in range(0, width, 2)
    ]
    bases = [
        pltpu.make_async_copy(source, result.at[unit], base_sem.at[unit])
        for unit, source in enumerate((inc.at[1], forc.at[1], inc.at[0], forc.at[0]))
    ]

    barrier = pltpu.get_barrier_semaphore()
    for to, condition in ((sec, None), (sec + 1, has_next), (sec - 1, has_previous)):
        for t in (east, west) if condition is None else (east, west, tile):
            @when(condition)
            def _():
                pl.semaphore_signal(barrier, inc=1, device_id=(to, t), device_id_type=MESH)

    def remote(source, target, sems, at, device):
        return pltpu.make_async_remote_copy(
            src_ref=source, dst_ref=target, send_sem=sems[0].at[at], recv_sem=sems[1].at[at],
            device_id=device, device_id_type=MESH,
        )

    def wind_copies(unit, window, section, parts):
        to = {0: east, 1: tile, 2: west}
        return [
            remote(wind.at[window], winds.at[unit, pl.ds(8 * part, 8)], (wsend, wrecv), (unit, part), (section, to[part]))
            for part in parts
        ]

    def halo(unit, source, section, part, first, count):
        if part == 0:
            at, column, to = STEPS - first - count, width - first - count, east
        else:
            at, column, to = STEPS + width + first, first, west
        return remote(
            source.at[pl.ds(column, count)], state.at[unit, pl.ds(at, count)], (send, recv), (unit, at), (section, to)
        )

    def start_of(unit, source, section, at):
        return remote(
            source.at[pl.ds(at, 2)], state.at[unit, pl.ds(STEPS + at, 2)], (send, recv), (unit, STEPS + at), (section, tile)
        )

    def pair(unit, j):
        source, to, sends = (
            (inc.at[0], sec, None), (forc.at[0], sec - 1, has_previous), (inc.at[1], sec + 1, has_next), (forc.at[1], sec, None)
        )[unit]
        return [(halo(unit, source, to, part, j - 1, 1), sends) for part in (0, 1)]

    def far(at):
        source = (inc.at[0], forc.at[1])[at]
        return [
            (remote(source.at[column], last.at[at, part], (last_sem.at[0], last_sem.at[1]), (at, part), (sec, to)), None)
            for part, column, to in ((0, width - STEPS, east), (1, STEPS - 1, west))
        ]

    small = [(c, None) for c in wind_copies(0, 0, sec, (0, 2)) + wind_copies(3, 1, sec, (0, 2))]
    small += [(c, has_previous) for c in wind_copies(1, 0, sec - 1, (1, 0, 2))]
    small += [(c, has_next) for c in wind_copies(2, 1, sec + 1, (1, 0, 2))]
    starts = [
        [(start_of(1, forc.at[0], sec - 1, at), has_previous), (start_of(2, inc.at[1], sec + 1, at), has_next)]
        for at in range(0, width, 2)
    ]
    order = [(unit, j) for j in range(1, STEPS + 1) for unit in (1, 2)]
    order += [(unit, j) for j in range(1, STEPS) for unit in (0, 3)]
    farthest = [far(0), far(1)]
    pairs = [pair(unit, j) for unit, j in order] + farthest

    def launch(group):
        for c, sends in group:
            @when(sends)
            def _():
                c.start()

    def leave(group):
        for c, sends in group:
            @when(sends)
            def _():
                c.wait_send()

    for c in local + bases:
        c.start()
    pl.semaphore_wait(barrier, 8 - 3 * ((sec + 1) // sections) - 3 * ((sections - sec) // sections))
    launch(small)
    for at, group in enumerate(pairs[:FIRST]):
        if at % 2 == 0 and at // 2 < len(starts):
            launch(starts[at // 2])
        launch(group)

    for at, matrix in enumerate((coupling[...].T, coupling[...])):
        high, low = halves(matrix)
        matrices[2 * at] = high
        matrices[2 * at + 1] = low
    zero = jnp.zeros((lats, size), jnp.float32)
    for unit in (0, 3):
        state[unit, 0] = zero
        state[unit, wide - 1] = zero
    winds[0, pl.ds(8, 8)] = wind[0]
    winds[3, pl.ds(8, 8)] = wind[1]

    def active(unit):
        return jnp.logical_not(((unit == 1) & (sec == sections - 1)) | ((unit == 2) & (sec == 0)))

    def wait_wind(unit, part):
        remote(wind.at[0], winds.at[unit, pl.ds(8 * part, 8)], (wsend, wrecv), (unit, part), (sec, east)).wait_recv()

    def spread(unit, _):
        @pl.when(active(unit))
        def _():
            wait_wind(unit, 0)
            wait_wind(unit, 2)

            @pl.when((unit == 1) | (unit == 2))
            def _():
                wait_wind(unit, 1)

            turned = winds[unit].T * jnp.where(unit % 2 == 0, 1.0, -1.0)
            for column in range(wide):
                speed[unit, column] = jnp.broadcast_to(turned[:, column + 4 : column + 5], (lats, 128))
        return 0

    lax.fori_loop(0, 4, spread, 0)

    lat = lax.broadcasted_iota(jnp.int32, (lats, size), 0)

    def flow(unit, column):
        return jnp.concatenate([speed[unit, column]] * (size // 128), 1)

    def update(units, step, column):
        before, after = level(step - 1), level(step)
        columns = (column, wide - 1 - column)
        centres = [[state[unit, before + at] for at in columns] for unit in units]
        mixed = []
        for way, centre in enumerate(centres):
            high, low = halves(jnp.concatenate(centre, 0))
            coarse, fine = matrices[2 * way], matrices[2 * way + 1]
            mixed.append(dot(high, coarse) + dot(low, coarse) + dot(high, fine))
        values = []
        for way, unit in enumerate(units):
            for i, at in enumerate(columns):
                x = centres[way][i]
                north = jnp.where(lat == lats - 1, 0.0, pltpu.roll(x, lats - 1, 0))
                south = jnp.where(lat == 0, 0.0, pltpu.roll(x, 1, 0))
                value = (
                    (1 - 2 * DIFFUSION) * x
                    + mixed[way][i * lats : (i + 1) * lats]
                    + flow(unit, at - way) * state[unit, before + at - 1]
                    - flow(unit, at + way) * state[unit, before + at + 1]
                    + DIFFUSION * (north + south)
                )
                values.append((unit, at, value))

        @pl.when(step < STEPS)
        def _():
            for unit, at, value in values:
                state[unit, after + at] = value

        @pl.when(step == STEPS)
        def _():
            for unit, at, value in values:
                result[unit, at - STEPS] -= jnp.where(active(unit), value, 0.0)

    def outgoing(unit):
        target = (model.at[1], adjoint.at[1], model.at[0], adjoint.at[0])[unit]
        return pltpu.make_async_copy(result.at[unit], target, out_sem.at[unit])

    for c in bases:
        c.wait()
    half = wide // 2

    def arrive(unit, at, count):
        remote(
            inc.at[0, pl.ds(0, count)], state.at[unit, pl.ds(at, count)], (send, recv), (unit, at), (sec, east)
        ).wait_recv()

    def event(number, _):
        moved = (number >= 1) & (number <= STEPS)
        units = (jnp.where(moved, 2, 0), jnp.where(moved, 1, 3))
        j = jnp.where(number > STEPS, number - STEPS, number)
        opens = number <= 1
        for unit in units:
            @pl.when(active(unit))
            def _():
                @pl.when(opens)
                def _():
                    for at in range(STEPS, STEPS + width, 2):
                        arrive(unit, at, 2)

                @pl.when((j > 0) & (number < 2 * STEPS))
                def _():
                    arrive(unit, STEPS - j, 1)
                    arrive(unit, STEPS + width - 1 + j, 1)

        for at, numbers in LATER:
            @pl.when(number == at + 1)
            def _():
                for follower in numbers:
                    launch(pairs[follower])

        def wave(q, _):
            def steps(step, _):
                def columns(column, _):
                    update(units, step, column)
                    return 0

                first = STEPS - q + step
                return lax.fori_loop(first, jnp.where(q == 0, half, first + 1), columns, 0)

            return lax.fori_loop(1, STEPS + 1, steps, 0)

        lax.fori_loop(jnp.where(opens, 0, j), j + 1, wave, 0)

        @pl.when(number == STEPS)
        def _():
            outgoing(1).start()
            outgoing(2).start()

        return 0

    lax.fori_loop(0, 2 * STEPS + 1, event, 0)

    for at, unit in enumerate((0, 3)):
        for part in (0, 1):
            first = -at if part == 0 else at
            reach = functools.reduce(
                jnp.multiply, [flow(unit, (step if part == 0 else wide - 1 - step) + first) for step in range(1, STEPS + 1)]
            )
            farthest[at][part][0].wait_recv()
            result[unit, 0 if part == 0 else width - 1] -= reach * last[at, part]
        outgoing(unit).start()

    for group in [small, *starts, *pairs]:
        leave(group)
    for unit in range(4):
        outgoing(unit).wait()


def solution(mesh):
    def body(increments, adjoint_forcing, wind, coupling):
        _, width, lats, size = increments.shape
        wide = width + 2 * STEPS
        any_space = pl.BlockSpec(memory_space=pl.ANY)
        vmem = pl.BlockSpec(memory_space=pltpu.VMEM)
        shape = jax.ShapeDtypeStruct(increments.shape, jnp.float32)
        return pl.pallas_call(
            kernel,
            out_shape=(shape, shape),
            in_specs=[any_space, any_space, vmem, vmem],
            out_specs=(any_space, any_space),
            scratch_shapes=[
                pltpu.VMEM((4, level(STEPS - 1) + wide - STEPS + 1, lats, size), jnp.float32),
                pltpu.VMEM((4, width, lats, size), jnp.float32),
                pltpu.VMEM((2, 2, lats, size), jnp.float32),
                pltpu.VMEM((4, 3 * width, lats), jnp.float32),
                pltpu.VMEM((4, wide, lats, 128), jnp.float32),
                pltpu.VMEM((4, size, size), jnp.bfloat16),
                pltpu.SemaphoreType.DMA((4, wide)),
                pltpu.SemaphoreType.DMA((4, wide)),
                pltpu.SemaphoreType.DMA((4, 3)),
                pltpu.SemaphoreType.DMA((4, 3)),
                pltpu.SemaphoreType.DMA((4,)),
                pltpu.SemaphoreType.DMA((4,)),
                pltpu.SemaphoreType.DMA((2, 2, 2)),
            ],
            compiler_params=pltpu.CompilerParams(
                collective_id=0, has_side_effects=True, vmem_limit_bytes=58 * 2**20
            ),
        )(increments, adjoint_forcing, wind, coupling)

    in_specs = (
        P("sec", "tile", None, None),
        P("sec", "tile", None, None),
        P("sec", "tile", None),
        P(),
    )
    out_specs = (P("sec", "tile", None, None), P("sec", "tile", None, None))
    return jax.shard_map(body, mesh=mesh, in_specs=in_specs, out_specs=out_specs, check_vma=False)
```
